256 devices in a mesh: rows: 32 (over y, z), cols: 8 (over x, core).
Axes of the slice: x: 4, y: 4, z: 8, core: 2. Of those that a mesh axis runs over, the one named last changes fastest.
Arguments:
- tensor_slab: float32 [8, 8192, 8192], P(None, 'rows', 'cols'), may hold values from -1536 to 1536
- prior_second: float32 [8192, 256], P(('cols', 'rows'))
- third_factor: float32 [8, 256], replicated, may hold values from -6 to 6
Outputs:
- first_factor: float32 [8192, 256], P(('rows', 'cols'))
- second_factor: float32 [8192, 256], P(('cols', 'rows'))
The draws below stay inside these ranges and needn't reach their ends.
All inputs are finite; a program needn't handle non-finite values.
Results may differ from the reference program's by a relative error of at most 0.00011.
Values sent between devices are 32-bit elements; how exact they have to be, the bound alone decides.
No kernel may reach another device: no remote copies, remote signals or barrier semaphores. Data moves between devices by JAX's collectives and lax.ppermute only.
A program may use at most 64 MiB of HBM per device.

```python
import jax
import jax.numpy as jnp
from jax import lax

R = 256
K = 8
NI = 8192
NJ = 8192


def draw_prior_second(key, part):
    key = jax.random.fold_in(key, 11)
    key_row, key_col, key_base = jax.random.split(key, 3)
    position = jnp.arange(NJ, dtype=jnp.float32) / (NJ - 1)
    row_scale = 10.0 ** jax.random.uniform(key_row, (NJ, 1), jnp.float32) * (1.0 + 2.0 * position[:, None]) / 9.6
    col_scale = 10.0 ** jax.random.uniform(key_col, (1, R), jnp.float32) / 3.0
    base = jax.random.normal(key_base, (NJ, R), jnp.float32)
    return (base * row_scale * col_scale).astype(jnp.float32)


def shard_levels(stream_key, extent, cuts, smallest, high):
    factor_of = 1.0
    for dim, shards_of in cuts:
        heights = jax.random.uniform(jax.random.fold_in(jax.random.fold_in(stream_key, 6), dim), (shards_of,), jnp.float32, smallest / len(cuts), high / len(cuts))
        factor_of = factor_of * jnp.repeat(jnp.exp(heights), extent[dim] // shards_of).reshape((-1,) + (1,) * (len(extent) - 1 - dim))
    return factor_of


def bell_draw(own_key, shape, spread, limit, cuts=(), held_as=jnp.bfloat16):
    entries = jax.random.normal(own_key, shape, jnp.float32) * spread
    if len(cuts) > 0:
        entries = shard_levels(own_key, shape, cuts, -0.22, 0.18) * entries
    return jnp.clip(entries, min=-limit, max=limit).astype(held_as)


def setup_inputs(seed: int = 0) -> dict:
    key_list = jax.random.split(jax.random.key(seed), 4)
    return {
        "tensor_slab": bell_draw(key_list[0], (K, NI, NJ), ((NI * K) ** 0.5), 1536.0, ((1, 32), (2, 8)), jnp.float32),
        "prior_second": draw_prior_second(jax.random.fold_in(key_list[3], 71), 0),
        "third_factor": bell_draw(key_list[2], (K, R), 1.0, 6.0, (), jnp.float32),
    }


def solve_rows(system, right):
    chol = jnp.linalg.cholesky(system)
    return jax.scipy.linalg.cho_solve((chol, True), right.T).T

def reference(tensor_slab, prior_second, third_factor):
    high = lax.Precision.HIGHEST
    third_gram = jnp.dot(third_factor.T.astype(jnp.float32), third_factor.astype(jnp.float32), precision=high, preferred_element_type=jnp.float32)
    first_mttkrp = jnp.zeros((NI, R), jnp.float32)
    for slab in range(K):
        scaled = prior_second * third_factor[slab][None, :]
        first_mttkrp = first_mttkrp + jnp.dot(tensor_slab[slab].astype(jnp.float32), scaled.astype(jnp.float32), precision=high, preferred_element_type=jnp.float32)
    first_system = jnp.dot(prior_second.T.astype(jnp.float32), prior_second.astype(jnp.float32), precision=high, preferred_element_type=jnp.float32) * third_gram
    first_factor = solve_rows(first_system, first_mttkrp)
    second_mttkrp = jnp.zeros((NJ, R), jnp.float32)
    for slab in range(K):
        scaled = first_factor * third_factor[slab][None, :]
        second_mttkrp = second_mttkrp + jnp.dot(tensor_slab[slab].T.astype(jnp.float32), scaled.astype(jnp.float32), precision=high, preferred_element_type=jnp.float32)
    second_system = jnp.dot(first_factor.T.astype(jnp.float32), first_factor.astype(jnp.float32), precision=high, preferred_element_type=jnp.float32) * third_gram
    second_factor = solve_rows(second_system, second_mttkrp)
    return (first_factor, second_factor)
```

```python
import functools

import jax
import jax.numpy as jnp
from jax import lax
from jax.experimental import pallas as pl
from jax.experimental.pallas import tpu as pltpu
from jax.sharding import PartitionSpec as P

R = 256
B = 32
NB = 16
Y, Z, X = 4, 8, 4
Z_GROUPS = [[y * Z + z for z in range(Z)] for y in range(Y)]


def split3(x):
    a = x.astype(jnp.bfloat16)
    rest = x - a.astype(jnp.float32)
    b = rest.astype(jnp.bfloat16)
    return a, b, (rest - b.astype(jnp.float32)).astype(jnp.bfloat16)


def tdot(x, y):
    x1, x2, x3 = split3(x)
    y1, y2, y3 = split3(y)
    left = jnp.concatenate([x1, x1, x2, x2, x1, x3], 0)
    right = jnp.concatenate([y1, y2, y1, y2, y3, y1], 0)
    return lax.dot_general(
        left, right, (((0,), (0,)), ((), ())), preferred_element_type=jnp.float32
    )


def sweep_columns(columns):
    rows = lax.broadcasted_iota(jnp.int32, (NB, 128), 0)
    for j in range(NB):
        own = columns[j]
        inverse = 1.0 / jnp.broadcast_to(own[j : j + 1, :], (NB, 128))
        at = rows == j
        own = jnp.where(at, -1.0, own)
        after = []
        for k in range(NB):
            if k == j:
                after.append(own * inverse)
                continue
            entry = jnp.broadcast_to(columns[k][j : j + 1, :], (NB, 128))
            after.append(jnp.where(at, 0.0, columns[k]) - (own * entry) * inverse)
        columns = after
    return columns


def invert_block(d):
    lane = lax.broadcasted_iota(jnp.int32, (B, 128), 1)
    row = lax.broadcasted_iota(jnp.int32, (B, 128), 0)
    for lo in range(0, B, NB):
        wide = [jnp.broadcast_to(d[:, lo + k : lo + k + 1], (B, 128)) for k in range(NB)]
        columns = sweep_columns([w[lo : lo + NB] for w in wide])
        inside = (lane >= lo) & (lane < lo + NB)
        panel = jnp.where(inside, jnp.where(lane == row, 1.0, 0.0), -d)[lo : lo + NB]
        y = jnp.zeros((NB, 128), jnp.float32)
        for k in range(NB):
            y = y + columns[k] * jnp.broadcast_to(panel[k : k + 1, :], (NB, 128))
        d = jnp.where(inside, 0.0, d)
        for k in range(NB):
            d = d - wide[k] * jnp.broadcast_to(y[k : k + 1, :], (B, 128))
        d = jnp.concatenate([part for part in (d[:lo], y, d[lo + NB :]) if part.shape[0]], 0)
    return d


def inverse_kernel(gram_ref, third_ref, out_ref, a_ref):
    a_ref[...] = gram_ref[...] * third_ref[...]
    lane = lax.broadcasted_iota(jnp.int32, (B, R), 1)
    row = lax.broadcasted_iota(jnp.int32, (B, R), 0)
    lanes = lax.broadcasted_iota(jnp.int32, (R, R), 1)
    for lo in range(0, R, B):
        panel = a_ref[lo : lo + B, :]
        half = lo // 128 * 128
        block = panel[:, half : half + 128]
        if lo > half:
            block = pltpu.roll(block, 128 - (lo - half), 1)
        pivot = invert_block(block)[:, :B]
        inside = (lane >= lo) & (lane < lo + B)
        y = tdot(pivot, jnp.where(inside, jnp.where(lane - lo == row, 1.0, 0.0), -panel))
        a_ref[...] = jnp.where((lanes >= lo) & (lanes < lo + B), 0.0, a_ref[...]) - tdot(panel, y)
        a_ref[lo : lo + B, :] = y
    out_ref[...] = -a_ref[...]


def system_inverse(gram, third_gram):
    return pl.pallas_call(
        inverse_kernel,
        out_shape=jax.ShapeDtypeStruct((R, R), jnp.float32),
        in_specs=[pl.BlockSpec(memory_space=pltpu.VMEM)] * 2,
        out_specs=pl.BlockSpec(memory_space=pltpu.VMEM),
        scratch_shapes=[pltpu.VMEM((R, R), jnp.float32)],
        cost_estimate=pl.CostEstimate(flops=2 * R**3, bytes_accessed=12 * R * R, transcendentals=0),
        name="system_inverse",
    )(gram, third_gram)


def shift_y(x, k):
    return lax.ppermute(x, "rows", [(i, (i // Z + k) % Y * Z + i % Z) for i in range(Y * Z)])


def shift_z(x, k):
    return lax.ppermute(x, "rows", [(i, i // Z * Z + (i % Z + k) % Z) for i in range(Y * Z)])


def shift_x(x, k):
    return lax.ppermute(x, "cols", [(i, (i // 2 + k) % X * 2 + i % 2) for i in range(2 * X)])


def swap_x(x, partner):
    return lax.ppermute(x, "cols", [(i, partner[i // 2] * 2 + i % 2) for i in range(2 * X)])


def swap_core(x):
    return lax.ppermute(x, "cols", [(i, i ^ 1) for i in range(2 * X)])


def sum_cols(x, core):
    half = R // 2
    own = lax.dynamic_slice_in_dim(x, core * half, half, 0)
    other = lax.dynamic_slice_in_dim(x, (1 - core) * half, half, 0)
    own = own + swap_core(other)
    own = own + swap_x(own, (1, 0, 3, 2))
    own = own + swap_x(own, (3, 2, 1, 0))
    other = swap_core(own)
    return lax.select(
        core == 0, jnp.concatenate([own, other], 0), jnp.concatenate([other, own], 0)
    )


def turned(blocks, start):
    n, size = len(blocks), blocks[0].shape[0]
    return lax.dynamic_slice_in_dim(jnp.concatenate(blocks + blocks[:-1], 0), start * size, n * size, 0)


def local(tensor_slab, prior_second, third_factor):
    high, highest = lax.Precision.HIGH, lax.Precision.HIGHEST
    dot = functools.partial(jnp.dot, precision=highest, preferred_element_type=jnp.float32)
    y = lax.axis_index("rows") // Z
    x, core = lax.axis_index("cols") // 2, lax.axis_index("cols") % 2
    third_gram = dot(third_factor.T, third_factor)

    mine = lax.all_to_all(
        jnp.tile(prior_second, (Z, 1)), "rows", 0, 0, tiled=True, axis_index_groups=Z_GROUPS
    )
    around = [mine, shift_y(mine, -1), shift_y(mine, 2), shift_y(mine, 1)]
    second = turned(around, (Y - y) % Y)

    gram = sum_cols(dot(second.T, second), core)
    slabs = jnp.einsum(
        "kin,nr->kir", tensor_slab, second, precision=high, preferred_element_type=jnp.float32
    )
    first_mttkrp = sum_cols(jnp.sum(slabs * third_factor[:, None, :], 0), core)
    first_block = dot(first_mttkrp, system_inverse(gram, third_gram))
    first_own = lax.dynamic_slice_in_dim(first_block, lax.axis_index("cols") * 32, 32, 0)

    part = core * 4 + x
    chunk = dot(lax.dynamic_slice_in_dim(first_block, part * 32, 32, 1).T, first_block)
    chunk = chunk + shift_y(chunk, 1) + shift_y(chunk, -1) + shift_y(chunk, 2)
    up, down = shift_z(chunk, 1), shift_z(chunk, -1)
    chunk = up + chunk + down + shift_z(up + chunk + down, 3) + shift_z(up + chunk, -3)
    half = turned([chunk, shift_x(chunk, -1), shift_x(chunk, 2), shift_x(chunk, 1)], (X - x) % X)
    other = swap_core(half)
    gram = lax.select(
        core == 0, jnp.concatenate([half, other], 0), jnp.concatenate([other, half], 0)
    )

    scaled = first_block[None, :, :] * third_factor[:, None, :]
    sums = jnp.einsum(
        "kin,kir->nr", tensor_slab, scaled, precision=high, preferred_element_type=jnp.float32
    )
    parts = jnp.split(turned(jnp.split(sums, Y, 0), y), Y, 0)
    part_sums = parts[0] + shift_y(parts[1], 1) + shift_y(parts[2], 2) + shift_y(parts[3], -1)
    pieces = lax.all_to_all(part_sums, "rows", 0, 0, tiled=True, axis_index_groups=Z_GROUPS)
    second_mttkrp = jnp.sum(pieces.reshape(Z, 32, R), 0)
    second_factor = dot(second_mttkrp, system_inverse(gram, third_gram))
    return (first_own, second_factor)


def solution(mesh):
    return jax.shard_map(
        local,
        mesh=mesh,
        in_specs=(P(None, "rows", "cols"), P(("cols", "rows"), None), P()),
        out_specs=(P(("rows", "cols"), None), P(("cols", "rows"), None)),
        check_vma=False,
    )
```

```python
import functools

import jax
import jax.numpy as jnp
from jax import lax
from jax.experimental import pallas as pl
from jax.experimental.pallas import tpu as pltpu
from jax.sharding import PartitionSpec as P

R = 256
K = 8
B = 32
NB = 16
Y, Z, X = 4, 8, 4
Z_GROUPS = [[y * Z + z for z in range(Z)] for y in range(Y)]


def split3(x):
    a = x.astype(jnp.bfloat16)
    rest = x - a.astype(jnp.float32)
    b = rest.astype(jnp.bfloat16)
    return a, b, (rest - b.astype(jnp.float32)).astype(jnp.bfloat16)


def tdot(x, y):
    x1, x2, x3 = split3(x)
    y1, y2, y3 = split3(y)
    left = jnp.concatenate([x1, x1, x2, x2, x1, x3], 0)
    right = jnp.concatenate([y1, y2, y1, y2, y3, y1], 0)
    return lax.dot_general(
        left, right, (((0,), (0,)), ((), ())), preferred_element_type=jnp.float32
    )


def sweep_columns(columns):
    rows = lax.broadcasted_iota(jnp.int32, (NB, 128), 0)
    for j in range(NB):
        own = columns[j]
        inverse = 1.0 / jnp.broadcast_to(own[j : j + 1, :], (NB, 128))
        at = rows == j
        own = jnp.where(at, -1.0, own)
        after = []
        for k in range(NB):
            if k == j:
                after.append(own * inverse)
                continue
            entry = jnp.broadcast_to(columns[k][j : j + 1, :], (NB, 128))
            after.append(jnp.where(at, 0.0, columns[k]) - (own * entry) * inverse)
        columns = after
    return columns


def invert_block(d):
    lane = lax.broadcasted_iota(jnp.int32, (B, 128), 1)
    row = lax.broadcasted_iota(jnp.int32, (B, 128), 0)
    for lo in range(0, B, NB):
        wide = [jnp.broadcast_to(d[:, lo + k : lo + k + 1], (B, 128)) for k in range(NB)]
        columns = sweep_columns([w[lo : lo + NB] for w in wide])
        inside = (lane >= lo) & (lane < lo + NB)
        panel = jnp.where(inside, jnp.where(lane == row, 1.0, 0.0), -d)[lo : lo + NB]
        y = jnp.zeros((NB, 128), jnp.float32)
        for k in range(NB):
            y = y + columns[k] * jnp.broadcast_to(panel[k : k + 1, :], (NB, 128))
        d = jnp.where(inside, 0.0, d)
        for k in range(NB):
            d = d - wide[k] * jnp.broadcast_to(y[k : k + 1, :], (B, 128))
        d = jnp.concatenate([part for part in (d[:lo], y, d[lo + NB :]) if part.shape[0]], 0)
    return d


BLOCK, CORE, COL, PART, TURN = range(5)


def half_rows(place_ref, own):
    core = place_ref[CORE]
    return pl.ds(pl.multiple_of((core if own else 1 - core) * 128, 128), 128)


def inverse_kernel(turned, place_ref, own_ref, other_ref, third_ref, out_ref, a_ref):
    core = place_ref[CORE]
    for side, ref in ((core, own_ref), (1 - core, other_ref)):
        for piece in range(4):
            slot = lax.rem(place_ref[TURN] + piece, 4) if turned else piece
            rows = pl.ds(pl.multiple_of(side * 128 + slot * 32, 32), 32)
            a_ref[rows, :] = ref[piece * 32 : piece * 32 + 32, :] * third_ref[rows, :]
    lane = lax.broadcasted_iota(jnp.int32, (B, R), 1)
    row = lax.broadcasted_iota(jnp.int32, (B, R), 0)
    lanes = lax.broadcasted_iota(jnp.int32, (R, R), 1)
    for lo in range(0, R, B):
        panel = a_ref[lo : lo + B, :]
        half = lo // 128 * 128
        block = panel[:, half : half + 128]
        if lo > half:
            block = pltpu.roll(block, 128 - (lo - half), 1)
        pivot = invert_block(block)[:, :B]
        inside = (lane >= lo) & (lane < lo + B)
        y = tdot(pivot, jnp.where(inside, jnp.where(lane - lo == row, 1.0, 0.0), -panel))
        a_ref[...] = jnp.where((lanes >= lo) & (lanes < lo + B), 0.0, a_ref[...]) - tdot(panel, y)
        a_ref[lo : lo + B, :] = y
    out_ref[...] = -a_ref[...]


def f32(*shape):
    return jax.ShapeDtypeStruct(shape, jnp.float32)


def bf16(*shape):
    return jax.ShapeDtypeStruct(shape, jnp.bfloat16)


def call(kernel, name, outs, args, scratch=()):
    out_specs = jax.tree.map(lambda _: pl.BlockSpec(memory_space=pltpu.VMEM), outs)
    return pl.pallas_call(
        kernel,
        out_shape=outs,
        in_specs=[pl.BlockSpec(memory_space=pltpu.SMEM)] + [pl.BlockSpec(memory_space=pltpu.VMEM)] * (len(args) - 1),
        out_specs=out_specs,
        scratch_shapes=list(scratch),
        compiler_params=pltpu.CompilerParams(vmem_limit_bytes=24 * 2**20),
        cost_estimate=pl.CostEstimate(flops=1024, bytes_accessed=1024, transcendentals=0),
        name=name,
    )(*args)


def system_inverse(place, own, other, third_gram, turned):
    return call(
        functools.partial(inverse_kernel, turned), "system_inverse", f32(R, R),
        (place, own, other, third_gram), [pltpu.VMEM((R, R), jnp.float32)],
    )


def split2(x):
    a = x.astype(jnp.bfloat16)
    return a, (x - a.astype(jnp.float32)).astype(jnp.bfloat16)


def dot(x, y):
    return jnp.dot(x, y, preferred_element_type=jnp.float32)


def dot6(x, y):
    x1, x2, x3 = split3(x)
    y1, y2, y3 = split3(y)
    return dot(jnp.concatenate([x1, x3, x2, x1, x2, x1], 1), jnp.concatenate([y3, y1, y2, y2, y1, y1], 0))


def prepare_kernel(slab_ref, third_ref, hi_ref, lo_ref, gram_ref, wide_ref):
    for block in range(Y):
        hi, lo = split2(slab_ref[0, :, block * R : block * R + R])
        hi_ref[block, 0] = hi
        lo_ref[block, 0] = lo

    @pl.when(pl.program_id(0) == 0)
    def _():
        third = third_ref[...]
        gram_ref[...] = lax.dot_general(
            third, third, (((0,), (0,)), ((), ())), precision=lax.Precision.HIGHEST,
            preferred_element_type=jnp.float32,
        )
        columns = third.T
        for k in range(K):
            wide_ref[k] = jnp.broadcast_to(columns[:, k : k + 1], (R, 128))


def prepare(slab, third):
    fixed = lambda *shape: pl.BlockSpec(shape, lambda k: (0,) * len(shape))
    parts = pl.BlockSpec((Y, 1, R, R), lambda k: (0, k, 0, 0))
    return pl.pallas_call(
        prepare_kernel,
        out_shape=[bf16(Y, K, R, R), bf16(Y, K, R, R), f32(R, R), f32(K, R, 128)],
        grid=(K,),
        in_specs=[pl.BlockSpec((1, R, Y * R), lambda k: (k, 0, 0)), fixed(K, R)],
        out_specs=[parts, parts, fixed(R, R), fixed(K, R, 128)],
        compiler_params=pltpu.CompilerParams(vmem_limit_bytes=24 * 2**20),
        cost_estimate=pl.CostEstimate(flops=1024, bytes_accessed=1024, transcendentals=0),
        name="prepare",
    )(slab, third)


def first_sums(place_ref, hi_ref, lo_ref, third_ref, blocks, total):
    for ahead, ref in blocks:
        block = lax.rem(place_ref[BLOCK] + ahead, Y)
        hi, lo = split2(ref[...])
        right = jnp.concatenate([hi, hi, lo], 0)
        for k in range(K):
            high, low = hi_ref[block, k], lo_ref[block, k]
            term = dot(jnp.concatenate([high, low, high], 1), right) * third_ref[k : k + 1, :]
            total = term if total is None else total + term
    return total


def own_sums_kernel(place_ref, hi_ref, lo_ref, third_ref, mine_ref, out_ref):
    out_ref[...] = first_sums(place_ref, hi_ref, lo_ref, third_ref, [(0, mine_ref)], None)


def rest_sums_kernel(
    place_ref, hi_ref, lo_ref, third_ref, after_ref, across_ref, before_ref, own_ref, out_ref, other_ref, sum_ref
):
    blocks = [(1, after_ref), (3, before_ref), (2, across_ref)]
    sum_ref[...] = first_sums(place_ref, hi_ref, lo_ref, third_ref, blocks, own_ref[...])
    out_ref[...] = sum_ref[half_rows(place_ref, True), :]
    other_ref[...] = sum_ref[half_rows(place_ref, False), :]


def own_gram_kernel(place_ref, mine_ref, out_ref):
    mine = mine_ref[...]
    out_ref[...] = dot6(mine.T, mine)


def rest_gram_kernel(place_ref, after_ref, across_ref, before_ref, own_ref, out_ref, other_ref, sum_ref):
    total = own_ref[...]
    for ref in (after_ref, before_ref, across_ref):
        block = ref[...]
        total = total + dot6(block.T, block)
    sum_ref[...] = total
    out_ref[...] = sum_ref[half_rows(place_ref, True), :]
    other_ref[...] = sum_ref[half_rows(place_ref, False), :]


def first_factor_kernel(
    place_ref, own_ref, other_ref, inverse_ref, wide_ref, hi_ref, lo_ref, chunk_ref, rows_ref, sum_ref
):
    sum_ref[half_rows(place_ref, True), :] = own_ref[...]
    sum_ref[half_rows(place_ref, False), :] = other_ref[...]
    factor = dot6(sum_ref[...], inverse_ref[...])
    sum_ref[...] = factor
    rows_ref[...] = sum_ref[pl.ds(pl.multiple_of(place_ref[COL] * 32, 32), 32), :]
    columns = factor.T
    sum_ref[...] = columns
    chunk_ref[...] = dot6(sum_ref[pl.ds(pl.multiple_of(place_ref[PART] * 32, 32), 32), :], factor)
    for k in range(K):
        wide = wide_ref[k]
        hi, lo = split2(columns * jnp.concatenate([wide, wide], 1))
        hi_ref[:, k * R : k * R + R] = hi
        lo_ref[:, k * R : k * R + R] = lo


def second_sums_kernel(ahead, place_ref, hi_ref, lo_ref, left_hi_ref, left_lo_ref, out_ref):
    block = lax.rem(place_ref[BLOCK] + ahead, Y)
    hi = hi_ref[block].reshape(K * R, R)
    lo = lo_ref[block].reshape(K * R, R)
    left = left_hi_ref[...]
    out_ref[...] = (dot(left, hi) + (dot(left_lo_ref[...], hi) + dot(left, lo))).T


def apply_kernel(place_ref, pieces_ref, inverse_ref, out_ref):
    total = pieces_ref[0:32, :]
    for k in range(1, Z):
        total = total + pieces_ref[32 * k : 32 * k + 32, :]
    out_ref[...] = dot6(total, inverse_ref[...])


def shift_y(x, k):
    return lax.ppermute(x, "rows", [(i, (i // Z + k) % Y * Z + i % Z) for i in range(Y * Z)])


def shift_z(x, k):
    return lax.ppermute(x, "rows", [(i, i // Z * Z + (i % Z + k) % Z) for i in range(Y * Z)])


def shift_x(x, k):
    return lax.ppermute(x, "cols", [(i, (i // 2 + k) % X * 2 + i % 2) for i in range(2 * X)])


def swap_x(x, partner):
    return lax.ppermute(x, "cols", [(i, partner[i // 2] * 2 + i % 2) for i in range(2 * X)])


def swap_core(x):
    return lax.ppermute(x, "cols", [(i, i ^ 1) for i in range(2 * X)])


def sum_cols(own, other):
    own = own + swap_core(other)
    own = own + swap_x(own, (1, 0, 3, 2))
    own = own + swap_x(own, (3, 2, 1, 0))
    return own, swap_core(own)


def local(tensor_slab, prior_second, third_factor):
    y = lax.axis_index("rows") // Z
    col = lax.axis_index("cols")
    x, core = col // 2, col % 2
    place = jnp.stack([y, core, col, core * 4 + x, x]).astype(jnp.int32)
    square = [pltpu.VMEM((R, R), jnp.float32)]
    halves = [f32(R // 2, R)] * 2

    mine = lax.all_to_all(
        jnp.tile(prior_second, (Z, 1)), "rows", 0, 0, tiled=True, axis_index_groups=Z_GROUPS
    )
    hi, lo, third_gram, wide = prepare(tensor_slab, third_factor)
    around = shift_y(mine, -1), shift_y(mine, 2), shift_y(mine, 1)
    own_gram = call(own_gram_kernel, "own_gram", f32(R, R), (place, mine))
    own_sums = call(own_sums_kernel, "own_sums", f32(R, R), (place, hi, lo, third_factor, mine))
    gram = call(rest_gram_kernel, "rest_gram", halves, (place, *around, own_gram), square)
    sums = call(rest_sums_kernel, "rest_sums", halves, (place, hi, lo, third_factor, *around, own_sums), square)

    inverse = system_inverse(place, *sum_cols(*gram), third_gram, False)
    left_hi, left_lo, chunk, first_own = call(
        first_factor_kernel, "first_factor", [bf16(R, K * R), bf16(R, K * R), f32(32, R), f32(32, R)],
        (place, *sum_cols(*sums), inverse, wide), square,
    )

    chunk = chunk + shift_y(chunk, 1) + shift_y(chunk, -1) + shift_y(chunk, 2)
    up, down = shift_z(chunk, 1), shift_z(chunk, -1)
    chunk = up + chunk + down + shift_z(up + chunk + down, 3) + shift_z(up + chunk, -3)
    half = jnp.concatenate([chunk, shift_x(chunk, -1), shift_x(chunk, 2), shift_x(chunk, 1)], 0)

    sums_of = lambda ahead: call(
        functools.partial(second_sums_kernel, ahead), "second_sums", f32(R, R), (place, hi, lo, left_hi, left_lo)
    )
    far = shift_y(sums_of(2), 2)
    right = shift_y(sums_of(1), 1)
    left = shift_y(sums_of(3), -1)
    part_sums = sums_of(0) + far + right + left
    pieces = lax.all_to_all(part_sums, "rows", 0, 0, tiled=True, axis_index_groups=Z_GROUPS)
    inverse = system_inverse(place, half, swap_core(half), third_gram, True)
    return (first_own, call(apply_kernel, "apply", f32(32, R), (place, pieces, inverse)))


def solution(mesh):
    return jax.shard_map(
        local,
        mesh=mesh,
        in_specs=(P(None, "rows", "cols"), P(("cols", "rows"), None), P()),
        out_specs=(P(("rows", "cols"), None), P(("cols", "rows"), None)),
        check_vma=False,
    )
```

```python
import functools

import jax
import jax.numpy as jnp
from jax import lax
from jax.experimental import pallas as pl
from jax.experimental.pallas import tpu as pltpu
from jax.sharding import PartitionSpec as P

R = 256
K = 8
B = 64
NB = 16
Y, Z, X = 4, 8, 4
Z_GROUPS = [[y * Z + z for z in range(Z)] for y in range(Y)]


def split3(x):
    a = x.astype(jnp.bfloat16)
    rest = x - a.astype(jnp.float32)
    b = rest.astype(jnp.bfloat16)
    return a, b, (rest - b.astype(jnp.float32)).astype(jnp.bfloat16)


def tdot(x, y):
    x1, x2, x3 = split3(x)
    y1, y2, y3 = split3(y)
    left = jnp.concatenate([x1, x1, x2, x2, x1, x3], 0)
    right = jnp.concatenate([y1, y2, y1, y2, y3, y1], 0)
    return lax.dot_general(
        left, right, (((0,), (0,)), ((), ())), preferred_element_type=jnp.float32
    )


def sweep_columns(columns):
    rows = lax.broadcasted_iota(jnp.int32, (8, 128), 0)
    tiles = range(NB // 8)
    columns = [[c[8 * q : 8 * q + 8] for q in tiles] for c in columns]
    for j in range(NB):
        p, row = divmod(j, 8)
        at = rows == row
        own = columns[j]
        inverse = 1.0 / jnp.broadcast_to(own[p][row : row + 1, :], (8, 128))
        marked = [jnp.where(at, -1.0, own[q]) if q == p else own[q] for q in tiles]
        scaled = [jnp.where(at, -inverse, own[q] * inverse) if q == p else own[q] * inverse for q in tiles]
        after = []
        for k in range(NB):
            if k == j:
                after.append(scaled)
                continue
            entry = jnp.broadcast_to(columns[k][p][row : row + 1, :], (8, 128))
            rest = [jnp.where(at, 0.0, columns[k][q]) if q == p else columns[k][q] for q in tiles]
            if k == j + 1:
                after.append([rest[q] - (marked[q] * entry) * inverse for q in tiles])
            else:
                after.append([rest[q] - scaled[q] * entry for q in tiles])
        columns = after
    return [jnp.concatenate(c, 0) for c in columns]


def tree_sum(terms):
    while len(terms) > 1:
        pairs = [terms[i] + terms[i + 1] for i in range(0, len(terms) - 1, 2)]
        terms = pairs + terms[len(terms) - len(terms) % 2 :]
    return terms[0]


def combine(columns, rows):
    wide = columns[0].shape
    return tree_sum([columns[k] * jnp.broadcast_to(rows[k : k + 1, :], wide) for k in range(NB)])


def invert_block(d):
    lane = lax.broadcasted_iota(jnp.int32, (NB, 128), 1)
    row = lax.broadcasted_iota(jnp.int32, (NB, 128), 0)
    n = B // NB
    d = [d[NB * q : NB * q + NB] for q in range(n)]
    for p in range(n):
        spread = lambda rows: [
            jnp.broadcast_to(rows[:, p * NB + k : p * NB + k + 1], (NB, 128)) for k in range(NB)
        ]
        inside = (lane >= p * NB) & (lane < p * NB + NB)
        panel = jnp.where(inside, jnp.where(lane - p * NB == row, 1.0, 0.0), -d[p])
        y = combine(sweep_columns(spread(d[p])), panel)
        after = {p: y}
        for q in [(p + 1 + i) % n for i in range(n - 1)]:
            after[q] = jnp.where(inside, 0.0, d[q]) - combine(spread(d[q]), y)
        d = [after[q] for q in range(n)]
    return jnp.concatenate(d, 0)


BLOCK, CORE, COL = range(3)


def half_rows(place_ref, own):
    core = place_ref[CORE]
    return pl.ds(pl.multiple_of((core if own else 1 - core) * 128, 128), 128)


def eliminate(a_ref, blocks):
    lane = lax.broadcasted_iota(jnp.int32, (B, R), 1)
    row = lax.broadcasted_iota(jnp.int32, (B, R), 0)
    lanes = lax.broadcasted_iota(jnp.int32, (R, R), 1)

    def first_lanes(panel, lo):
        block = panel[:, lo // 128 * 128 : lo // 128 * 128 + 128]
        return pltpu.roll(block, 128 - lo % 128, 1) if lo % 128 else block

    panel = a_ref[blocks[0] : blocks[0] + B, :]
    for lo in blocks:
        pivot = invert_block(first_lanes(panel, lo))[:, :B]
        inside = (lane >= lo) & (lane < lo + B)
        y = tdot(pivot, jnp.where(inside, jnp.where(lane - lo == row, 1.0, 0.0), -panel))
        if lo + B in blocks:
            ahead = first_lanes(panel, lo + B)[:, :B]
            ahead = jnp.where(inside, 0.0, a_ref[lo + B : lo + 2 * B, :]) - tdot(ahead, y)
        a_ref[...] = jnp.where((lanes >= lo) & (lanes < lo + B), 0.0, a_ref[...]) - tdot(panel, y)
        a_ref[lo : lo + B, :] = y
        panel = ahead if lo + B in blocks else None


def inverse_start_kernel(place_ref, own_ref, other_ref, third_ref, out_ref, a_ref):
    for own, ref in ((True, own_ref), (False, other_ref)):
        rows = half_rows(place_ref, own)
        a_ref[rows, :] = ref[...] * third_ref[rows, :]
    eliminate(a_ref, range(0, R // 2, B))
    out_ref[...] = a_ref[...]


def inverse_end_kernel(place_ref, half_ref, out_ref, a_ref):
    a_ref[...] = half_ref[...]
    eliminate(a_ref, range(R // 2, R, B))
    out_ref[...] = -a_ref[...]


def f32(*shape):
    return jax.ShapeDtypeStruct(shape, jnp.float32)


def bf16(*shape):
    return jax.ShapeDtypeStruct(shape, jnp.bfloat16)


MICROSECONDS = {
    "own_gram": 1.0, "own_sums": 1.5, "rest_gram": 1.4, "rest_sums": 3.3, "cut": 0.5, "inverse_start": 5.0,
    "inverse_end": 5.0, "first_factor": 1.8, "second_sums": 1.6, "add": 0.5,
    "apply": 1.4,
}


def cost(us):
    return pl.CostEstimate(flops=int(us * 1.1e9), bytes_accessed=int(us * 3.6e6), transcendentals=0)


def call(kernel, name, outs, args, scratch=(), after=()):
    n = len(args)

    def body(*refs):
        kernel(*refs[:n], *refs[n + len(after) :])

    out_specs = jax.tree.map(lambda _: pl.BlockSpec(memory_space=pltpu.VMEM), outs)
    return pl.pallas_call(
        body,
        out_shape=outs,
        in_specs=[pl.BlockSpec(memory_space=pltpu.SMEM)]
        + [pl.BlockSpec(memory_space=pltpu.VMEM)] * (n - 1)
        + [pl.BlockSpec(memory_space=pl.ANY)] * len(after),
        out_specs=out_specs,
        scratch_shapes=list(scratch),
        compiler_params=pltpu.CompilerParams(vmem_limit_bytes=24 * 2**20),
        cost_estimate=cost(MICROSECONDS[name]),
        name=name,
    )(*args, *after)


SQUARE = [pltpu.VMEM((R, R), jnp.float32)]


def inverse_start(place, own, other, third_gram, after=()):
    return call(inverse_start_kernel, "inverse_start", f32(R, R), (place, own, other, third_gram), SQUARE, after)


def inverse_end(place, half, after=()):
    return call(inverse_end_kernel, "inverse_end", f32(R, R), (place, half), SQUARE, after)


def split2(x):
    a = x.astype(jnp.bfloat16)
    return a, (x - a.astype(jnp.float32)).astype(jnp.bfloat16)


def dot(x, y):
    return jnp.dot(x, y, preferred_element_type=jnp.float32)


def dot6(x, y):
    x1, x2, x3 = split3(x)
    y1, y2, y3 = split3(y)
    return dot(jnp.concatenate([x1, x3, x2, x1, x2, x1], 1), jnp.concatenate([y3, y1, y2, y2, y1, y1], 0))


def prepare_kernel(slab_ref, third_ref, after_ref, hi_ref, lo_ref, gram_ref, wide_ref):
    for block in range(Y):
        hi, lo = split2(slab_ref[0, :, block * R : block * R + R])
        hi_ref[block, 0] = hi
        lo_ref[block, 0] = lo

    @pl.when(pl.program_id(0) == 0)
    def _():
        third = third_ref[...]
        gram_ref[...] = lax.dot_general(
            third, third, (((0,), (0,)), ((), ())), precision=lax.Precision.HIGHEST,
            preferred_element_type=jnp.float32,
        )
        columns = third.T
        for k in range(K):
            wide_ref[k] = jnp.broadcast_to(columns[:, k : k + 1], (R, 128))


def prepare(slab, third, after):
    fixed = lambda *shape: pl.BlockSpec(shape, lambda k: (0,) * len(shape))
    parts = pl.BlockSpec((Y, 1, R, R), lambda k: (0, k, 0, 0))
    return pl.pallas_call(
        prepare_kernel,
        out_shape=[bf16(Y, K, R, R), bf16(Y, K, R, R), f32(R, R), f32(K, R, 128)],
        grid=(K,),
        in_specs=[pl.BlockSpec((1, R, Y * R), lambda k: (k, 0, 0)), fixed(K, R), pl.BlockSpec(memory_space=pl.ANY)],
        out_specs=[parts, parts, fixed(R, R), fixed(K, R, 128)],
        compiler_params=pltpu.CompilerParams(vmem_limit_bytes=24 * 2**20),
        cost_estimate=cost(2.5),
        name="prepare",
    )(slab, third, after)


def first_sums(place_ref, hi_ref, lo_ref, third_ref, blocks, total):
    for ahead, ref in blocks:
        block = lax.rem(place_ref[BLOCK] + ahead, Y)
        hi, lo = split2(ref[...])
        right = jnp.concatenate([hi, hi, lo], 0)
        for k in range(K):
            high, low = hi_ref[block, k], lo_ref[block, k]
            term = dot(jnp.concatenate([high, low, high], 1), right) * third_ref[k : k + 1, :]
            total = term if total is None else total + term
    return total


def own_sums_kernel(place_ref, hi_ref, lo_ref, third_ref, mine_ref, out_ref):
    out_ref[...] = first_sums(place_ref, hi_ref, lo_ref, third_ref, [(0, mine_ref)], None)


def rest_sums_kernel(
    place_ref, hi_ref, lo_ref, third_ref, after_ref, across_ref, before_ref, own_ref, out_ref
):
    blocks = [(1, after_ref), (3, before_ref), (2, across_ref)]
    out_ref[...] = first_sums(place_ref, hi_ref, lo_ref, third_ref, blocks, own_ref[...])


def own_gram_kernel(place_ref, mine_ref, out_ref):
    mine = mine_ref[...]
    out_ref[...] = dot6(mine.T, mine)


def rest_gram_kernel(place_ref, after_ref, across_ref, before_ref, own_ref, out_ref, other_ref, sum_ref):
    total = own_ref[...]
    for ref in (after_ref, before_ref, across_ref):
        block = ref[...]
        total = total + dot6(block.T, block)
    sum_ref[...] = total
    out_ref[...] = sum_ref[half_rows(place_ref, True), :]
    other_ref[...] = sum_ref[half_rows(place_ref, False), :]


def cut_kernel(place_ref, sum_ref, out_ref, other_ref):
    out_ref[...] = sum_ref[half_rows(place_ref, True), :]
    other_ref[...] = sum_ref[half_rows(place_ref, False), :]


def first_factor_kernel(
    place_ref, own_ref, other_ref, inverse_ref, wide_ref, hi_ref, lo_ref, chunk_ref, rows_ref, factor_ref, columns_ref
):
    factor_ref[half_rows(place_ref, True), :] = own_ref[...]
    factor_ref[half_rows(place_ref, False), :] = other_ref[...]
    factor = dot6(factor_ref[...], inverse_ref[...])
    factor_ref[...] = factor
    rows_ref[...] = factor_ref[pl.ds(pl.multiple_of(place_ref[COL] * 32, 32), 32), :]
    columns = factor.T
    columns_ref[...] = columns
    chunk_ref[...] = dot6(columns_ref[half_rows(place_ref, True), :], factor)
    for k in range(K):
        wide = wide_ref[k]
        hi, lo = split2(columns * jnp.concatenate([wide, wide], 1))
        hi_ref[:, k * R : k * R + R] = hi
        lo_ref[:, k * R : k * R + R] = lo


def second_sums_kernel(ahead, place_ref, hi_ref, lo_ref, left_hi_ref, left_lo_ref, out_ref):
    block = lax.rem(place_ref[BLOCK] + ahead, Y)
    hi = hi_ref[block].reshape(K * R, R)
    lo = lo_ref[block].reshape(K * R, R)
    left = left_hi_ref[...]
    out_ref[...] = (dot(left, hi) + (dot(left_lo_ref[...], hi) + dot(left, lo))).T


def add_kernel(place_ref, *refs):
    refs[-1][...] = tree_sum([ref[...] for ref in refs[:-1]])


def add(place, *terms, after=()):
    return call(add_kernel, "add", f32(*terms[0].shape), (place, *terms), (), after)


def apply_kernel(place_ref, pieces_ref, inverse_ref, out_ref):
    total = tree_sum([pieces_ref[32 * k : 32 * k + 32, :] for k in range(Z)])
    out_ref[...] = dot6(total, inverse_ref[...])


def shift_y(x, k):
    return lax.ppermute(x, "rows", [(i, (i // Z + k) % Y * Z + i % Z) for i in range(Y * Z)])


def shift_z(x, k):
    return lax.ppermute(x, "rows", [(i, i // Z * Z + (i % Z + k) % Z) for i in range(Y * Z)])


def shift_x(x, k):
    return lax.ppermute(x, "cols", [(i, (i // 2 + k) % X * 2 + i % 2) for i in range(2 * X)])


def swap_x(x, partner):
    return lax.ppermute(x, "cols", [(i, partner[i // 2] * 2 + i % 2) for i in range(2 * X)])


def swap_y(x, partner):
    return lax.ppermute(x, "rows", [(i, partner[i // Z] * Z + i % Z) for i in range(Y * Z)])


def swap_core(x):
    return lax.ppermute(x, "cols", [(i, i ^ 1) for i in range(2 * X)])


def local(tensor_slab, prior_second, third_factor):
    y = lax.axis_index("rows") // Z
    col = lax.axis_index("cols")
    core = col % 2
    place = jnp.stack([y, core, col]).astype(jnp.int32)
    halves = [f32(R // 2, R)] * 2
    even, odd = (1, 0, 3, 2), (3, 2, 1, 0)

    mine = lax.all_to_all(
        jnp.tile(prior_second, (Z, 1)), "rows", 0, 0, tiled=True, axis_index_groups=Z_GROUPS
    )
    around = shift_y(mine, -1), shift_y(mine, 2), shift_y(mine, 1)
    hi, lo, third_gram, wide = prepare(tensor_slab, third_factor, mine)
    own_gram = call(own_gram_kernel, "own_gram", f32(R, R), (place, mine))
    own_sums = call(own_sums_kernel, "own_sums", f32(R, R), (place, hi, lo, third_factor, mine))

    gram, other = call(
        rest_gram_kernel, "rest_gram", halves, (place, *around, own_gram), SQUARE, (own_sums,)
    )
    gram = gram + swap_core(other)
    sums = call(rest_sums_kernel, "rest_sums", f32(R, R), (place, hi, lo, third_factor, *around, own_sums), (), (gram,))
    gram = gram + swap_x(gram, even)
    sums, other = call(cut_kernel, "cut", halves, (place, sums), (), (gram,))
    gram = gram + swap_x(gram, odd)
    sums = sums + swap_core(other)
    sums = sums + swap_x(sums, even)
    inverse = inverse_start(place, gram, swap_core(gram), third_gram, (sums,))
    sums = add(place, sums, swap_x(sums, odd), after=(inverse,))
    inverse = inverse_end(place, inverse, (sums,))
    left_hi, left_lo, chunk, first_own = call(
        first_factor_kernel, "first_factor", [bf16(R, K * R), bf16(R, K * R), f32(R // 2, R), f32(32, R)],
        (place, sums, swap_core(sums), inverse, wide), SQUARE * 2,
    )

    sums_of = lambda ahead, *after: call(
        functools.partial(second_sums_kernel, ahead), "second_sums", f32(R, R),
        (place, hi, lo, left_hi, left_lo), (), after,
    )
    far = sums_of(2)
    right = sums_of(1, far)
    left = sums_of(3, right)
    chunk = add(place, chunk, shift_y(chunk, 1), shift_y(chunk, -1), shift_y(chunk, 2), after=(left,))
    own = sums_of(0, chunk)
    below = shift_z(chunk, 1) + chunk
    above = below + shift_z(chunk, -1)
    chunk = above + shift_z(above, 3) + shift_z(below, -3)
    part_sums = own + shift_y(far, 2) + shift_y(right, 1) + shift_y(left, -1)
    pieces = lax.all_to_all(part_sums, "rows", 0, 0, tiled=True, axis_index_groups=Z_GROUPS)
    inverse = inverse_end(place, inverse_start(place, chunk, swap_core(chunk), third_gram))
    return first_own, call(apply_kernel, "apply", f32(32, R), (place, pieces, inverse))


def solution(mesh):
    return jax.shard_map(
        local,
        mesh=mesh,
        in_specs=(P(None, "rows", "cols"), P(("cols", "rows"), None), P()),
        out_specs=(P(("rows", "cols"), None), P(("cols", "rows"), None)),
        check_vma=False,
    )
```

```python
import functools

import jax
import jax.numpy as jnp
from jax import lax
from jax.experimental import pallas as pl
from jax.experimental.pallas import tpu as pltpu
from jax.sharding import PartitionSpec as P

R = 256
K = 8
B = 64
NB = 16
Y, Z, X = 4, 8, 4
Z_GROUPS = [[y * Z + z for z in range(Z)] for y in range(Y)]


def split3(x):
    a = x.astype(jnp.bfloat16)
    rest = x - a.astype(jnp.float32)
    b = rest.astype(jnp.bfloat16)
    return a, b, (rest - b.astype(jnp.float32)).astype(jnp.bfloat16)


def tdot(x, y):
    x1, x2, x3 = split3(x)
    y1, y2, y3 = split3(y)
    left = jnp.concatenate([x1, x1, x2, x2, x1, x3], 0)
    right = jnp.concatenate([y1, y2, y1, y2, y3, y1], 0)
    return lax.dot_general(
        left, right, (((0,), (0,)), ((), ())), preferred_element_type=jnp.float32
    )


def sweep_columns(columns):
    rows = lax.broadcasted_iota(jnp.int32, (8, 128), 0)
    tiles = range(NB // 8)
    columns = [[c[8 * q : 8 * q + 8] for q in tiles] for c in columns]
    for j in range(NB):
        p, row = divmod(j, 8)
        at = rows == row
        own = columns[j]
        inverse = 1.0 / jnp.broadcast_to(own[p][row : row + 1, :], (8, 128))
        marked = [jnp.where(at, -1.0, own[q]) if q == p else own[q] for q in tiles]
        scaled = [jnp.where(at, -inverse, own[q] * inverse) if q == p else own[q] * inverse for q in tiles]
        after = []
        for k in range(NB):
            if k == j:
                after.append(scaled)
                continue
            entry = jnp.broadcast_to(columns[k][p][row : row + 1, :], (8, 128))
            rest = [jnp.where(at, 0.0, columns[k][q]) if q == p else columns[k][q] for q in tiles]
            if k == j + 1:
                after.append([rest[q] - (marked[q] * entry) * inverse for q in tiles])
            else:
                after.append([rest[q] - scaled[q] * entry for q in tiles])
        columns = after
    return [jnp.concatenate(c, 0) for c in columns]


def tree_sum(terms):
    while len(terms) > 1:
        pairs = [terms[i] + terms[i + 1] for i in range(0, len(terms) - 1, 2)]
        terms = pairs + terms[len(terms) - len(terms) % 2 :]
    return terms[0]


def combine(columns, rows):
    wide = columns[0].shape
    return tree_sum([columns[k] * jnp.broadcast_to(rows[k : k + 1, :], wide) for k in range(NB)])


def invert_block(d):
    lane = lax.broadcasted_iota(jnp.int32, (NB, 128), 1)
    row = lax.broadcasted_iota(jnp.int32, (NB, 128), 0)
    n = B // NB
    d = [d[NB * q : NB * q + NB] for q in range(n)]
    for p in range(n):
        spread = lambda rows: [
            jnp.broadcast_to(rows[:, p * NB + k : p * NB + k + 1], (NB, 128)) for k in range(NB)
        ]
        inside = (lane >= p * NB) & (lane < p * NB + NB)
        panel = jnp.where(inside, jnp.where(lane - p * NB == row, 1.0, 0.0), -d[p])
        y = combine(sweep_columns(spread(d[p])), panel)
        after = {p: y}
        for q in [(p + 1 + i) % n for i in range(n - 1)]:
            after[q] = jnp.where(inside, 0.0, d[q]) - combine(spread(d[q]), y)
        d = [after[q] for q in range(n)]
    return jnp.concatenate(d, 0)


BLOCK, CORE, COL, SIDE = range(4)


def half_rows(place_ref, own):
    core = place_ref[CORE]
    return pl.ds(pl.multiple_of((core if own else 1 - core) * 128, 128), 128)


def eliminate(a_ref, blocks):
    lane = lax.broadcasted_iota(jnp.int32, (B, R), 1)
    row = lax.broadcasted_iota(jnp.int32, (B, R), 0)
    lanes = lax.broadcasted_iota(jnp.int32, (R, R), 1)

    def first_lanes(panel, lo):
        block = panel[:, lo // 128 * 128 : lo // 128 * 128 + 128]
        return pltpu.roll(block, 128 - lo % 128, 1) if lo % 128 else block

    panel = a_ref[blocks[0] : blocks[0] + B, :]
    for lo in blocks:
        pivot = invert_block(first_lanes(panel, lo))[:, :B]
        inside = (lane >= lo) & (lane < lo + B)
        y = tdot(pivot, jnp.where(inside, jnp.where(lane - lo == row, 1.0, 0.0), -panel))
        if lo + B in blocks:
            ahead = first_lanes(panel, lo + B)[:, :B]
            ahead = jnp.where(inside, 0.0, a_ref[lo + B : lo + 2 * B, :]) - tdot(ahead, y)
        a_ref[...] = jnp.where((lanes >= lo) & (lanes < lo + B), 0.0, a_ref[...]) - tdot(panel, y)
        a_ref[lo : lo + B, :] = y
        panel = ahead if lo + B in blocks else None


def quarter_rows(place_ref, own, first):
    core, side = place_ref[CORE], place_ref[SIDE]
    start = (core if own else 1 - core) * 128 + (side if first else 1 - side) * 64
    return pl.ds(pl.multiple_of(start, 64), 64)


def inverse_start_kernel(quarters, place_ref, own_ref, other_ref, third_ref, out_ref, a_ref):
    for own, ref in ((True, own_ref), (False, other_ref)):
        if quarters:
            for first in (True, False):
                rows = quarter_rows(place_ref, own, first)
                a_ref[rows, :] = ref[0 if first else 64 : 64 if first else 128, :] * third_ref[rows, :]
        else:
            rows = half_rows(place_ref, own)
            a_ref[rows, :] = ref[...] * third_ref[rows, :]
    eliminate(a_ref, range(0, R // 2, B))
    out_ref[...] = a_ref[...]


def inverse_end_kernel(place_ref, half_ref, out_ref, a_ref):
    a_ref[...] = half_ref[...]
    eliminate(a_ref, range(R // 2, R, B))
    out_ref[...] = -a_ref[...]


def f32(*shape):
    return jax.ShapeDtypeStruct(shape, jnp.float32)


def bf16(*shape):
    return jax.ShapeDtypeStruct(shape, jnp.bfloat16)


MICROSECONDS = {
    "own_gram": 1.0, "own_sums": 1.5, "rest_gram": 1.4, "rest_sums": 3.3, "cut": 0.5, "inverse_start": 5.0,
    "inverse_end": 5.0, "first_factor": 1.8, "second_sums": 1.6, "add": 0.5,
    "apply": 1.4,
}


def cost(us):
    return pl.CostEstimate(flops=int(us * 1.1e9), bytes_accessed=int(us * 3.6e6), transcendentals=0)


def call(kernel, name, outs, args, scratch=(), after=(), us=None):
    n = len(args)

    def body(*refs):
        kernel(*refs[:n], *refs[n + len(after) :])

    out_specs = jax.tree.map(lambda _: pl.BlockSpec(memory_space=pltpu.VMEM), outs)
    return pl.pallas_call(
        body,
        out_shape=outs,
        in_specs=[pl.BlockSpec(memory_space=pltpu.SMEM)]
        + [pl.BlockSpec(memory_space=pltpu.VMEM)] * (n - 1)
        + [pl.BlockSpec(memory_space=pl.ANY)] * len(after),
        out_specs=out_specs,
        scratch_shapes=list(scratch),
        compiler_params=pltpu.CompilerParams(vmem_limit_bytes=24 * 2**20),
        cost_estimate=cost(us or MICROSECONDS[name]),
        name=name,
    )(*args, *after)


SQUARE = [pltpu.VMEM((R, R), jnp.float32)]


def inverse_start(place, own, other, third_gram, quarters, after=(), us=None):
    return call(functools.partial(inverse_start_kernel, quarters), "inverse_start", f32(R, R), (place, own, other, third_gram), SQUARE, after, us)


def inverse_end(place, half, after=(), us=None):
    return call(inverse_end_kernel, "inverse_end", f32(R, R), (place, half), SQUARE, after, us)


def split2(x):
    a = x.astype(jnp.bfloat16)
    return a, (x - a.astype(jnp.float32)).astype(jnp.bfloat16)


def dot(x, y):
    return jnp.dot(x, y, preferred_element_type=jnp.float32)


def dot6(x, y):
    x1, x2, x3 = split3(x)
    y1, y2, y3 = split3(y)
    return dot(jnp.concatenate([x1, x3, x2, x1, x2, x1], 1), jnp.concatenate([y3, y1, y2, y2, y1, y1], 0))


def prepare_kernel(slab_ref, third_ref, after_ref, hi_ref, lo_ref, gram_ref, wide_ref):
    for block in range(Y):
        hi, lo = split2(slab_ref[0, :, block * R : block * R + R])
        hi_ref[block, 0] = hi
        lo_ref[block, 0] = lo

    @pl.when(pl.program_id(0) == 0)
    def _():
        third = third_ref[...]
        gram_ref[...] = lax.dot_general(
            third, third, (((0,), (0,)), ((), ())), precision=lax.Precision.HIGHEST,
            preferred_element_type=jnp.float32,
        )
        columns = third.T
        for k in range(K):
            wide_ref[k] = jnp.broadcast_to(columns[:, k : k + 1], (R, 128))


def prepare(slab, third, after):
    fixed = lambda *shape: pl.BlockSpec(shape, lambda k: (0,) * len(shape))
    parts = pl.BlockSpec((Y, 1, R, R), lambda k: (0, k, 0, 0))
    return pl.pallas_call(
        prepare_kernel,
        out_shape=[bf16(Y, K, R, R), bf16(Y, K, R, R), f32(R, R), f32(K, R, 128)],
        grid=(K,),
        in_specs=[pl.BlockSpec((1, R, Y * R), lambda k: (k, 0, 0)), fixed(K, R), pl.BlockSpec(memory_space=pl.ANY)],
        out_specs=[parts, parts, fixed(R, R), fixed(K, R, 128)],
        compiler_params=pltpu.CompilerParams(vmem_limit_bytes=24 * 2**20),
        cost_estimate=cost(2.5),
        name="prepare",
    )(slab, third, after)


def first_sums(place_ref, hi_ref, lo_ref, third_ref, blocks, total):
    for ahead, ref in blocks:
        block = lax.rem(place_ref[BLOCK] + ahead, Y)
        hi, lo = split2(ref[...])
        right = jnp.concatenate([hi, hi, lo], 0)
        for k in range(K):
            high, low = hi_ref[block, k], lo_ref[block, k]
            term = dot(jnp.concatenate([high, low, high], 1), right) * third_ref[k : k + 1, :]
            total = term if total is None else total + term
    return total


def own_sums_kernel(place_ref, hi_ref, lo_ref, third_ref, mine_ref, out_ref):
    out_ref[...] = first_sums(place_ref, hi_ref, lo_ref, third_ref, [(0, mine_ref)], None)


def rest_sums_kernel(
    place_ref, hi_ref, lo_ref, third_ref, after_ref, across_ref, before_ref, own_ref, out_ref
):
    blocks = [(1, after_ref), (3, before_ref), (2, across_ref)]
    out_ref[...] = first_sums(place_ref, hi_ref, lo_ref, third_ref, blocks, own_ref[...])


def own_gram_kernel(place_ref, mine_ref, out_ref):
    mine = mine_ref[...]
    out_ref[...] = dot6(mine.T, mine)


def rest_gram_kernel(place_ref, after_ref, across_ref, before_ref, own_ref, out_ref, other_ref, sum_ref):
    total = own_ref[...]
    for ref in (after_ref, before_ref, across_ref):
        block = ref[...]
        total = total + dot6(block.T, block)
    sum_ref[...] = total
    out_ref[...] = sum_ref[half_rows(place_ref, True), :]
    other_ref[...] = sum_ref[half_rows(place_ref, False), :]


def cut_kernel(place_ref, sum_ref, out_ref, other_ref):
    out_ref[...] = sum_ref[half_rows(place_ref, True), :]
    other_ref[...] = sum_ref[half_rows(place_ref, False), :]


def first_factor_kernel(
    place_ref, own_ref, other_ref, inverse_ref, wide_ref, left_ref, chunk_ref, rows_ref, factor_ref, columns_ref
):
    factor_ref[half_rows(place_ref, True), :] = own_ref[...]
    factor_ref[half_rows(place_ref, False), :] = other_ref[...]
    factor = dot6(factor_ref[...], inverse_ref[...])
    factor_ref[...] = factor
    rows_ref[...] = factor_ref[pl.ds(pl.multiple_of(place_ref[COL] * 32, 32), 32), :]
    columns = factor.T
    columns_ref[...] = columns
    chunk_ref[...] = dot6(columns_ref[quarter_rows(place_ref, True, True), :], factor)
    for k in range(K):
        wide = wide_ref[k]
        hi, lo = split2(columns * jnp.concatenate([wide, wide], 1))
        left_ref[:R, k * R : k * R + R] = hi
        left_ref[R:, k * R : k * R + R] = lo


def second_sums_kernel(ahead, place_ref, hi_ref, lo_ref, left_ref, out_ref):
    block = lax.rem(place_ref[BLOCK] + ahead, Y)
    by_hi = dot(left_ref[...], hi_ref[block].reshape(K * R, R))
    by_lo = dot(left_ref[:R, :], lo_ref[block].reshape(K * R, R))
    out_ref[...] = (by_hi[:R] + (by_hi[R:] + by_lo)).T


def add_kernel(place_ref, *refs):
    refs[-1][...] = tree_sum([ref[...] for ref in refs[:-1]])


def add(place, *terms, after=()):
    return call(add_kernel, "add", f32(*terms[0].shape), (place, *terms), (), after)


def apply_kernel(place_ref, pieces_ref, inverse_ref, out_ref):
    total = tree_sum([pieces_ref[32 * k : 32 * k + 32, :] for k in range(Z)])
    out_ref[...] = dot6(total, inverse_ref[...])


def shift_y(x, k):
    return lax.ppermute(x, "rows", [(i, (i // Z + k) % Y * Z + i % Z) for i in range(Y * Z)])


def shift_z(x, k):
    return lax.ppermute(x, "rows", [(i, i // Z * Z + (i % Z + k) % Z) for i in range(Y * Z)])


def shift_x(x, k):
    return lax.ppermute(x, "cols", [(i, (i // 2 + k) % X * 2 + i % 2) for i in range(2 * X)])


def swap_x(x, partner):
    return lax.ppermute(x, "cols", [(i, partner[i // 2] * 2 + i % 2) for i in range(2 * X)])


def swap_y(x, partner):
    return lax.ppermute(x, "rows", [(i, partner[i // Z] * Z + i % Z) for i in range(Y * Z)])


def swap_core(x):
    return lax.ppermute(x, "cols", [(i, i ^ 1) for i in range(2 * X)])


def local(tensor_slab, prior_second, third_factor):
    y = lax.axis_index("rows") // Z
    col = lax.axis_index("cols")
    core = col % 2
    place = jnp.stack([y, core, col, col // 2 % 2]).astype(jnp.int32)
    halves = [f32(R // 2, R)] * 2
    even, odd = (1, 0, 3, 2), (3, 2, 1, 0)

    mine = lax.all_to_all(
        jnp.tile(prior_second, (Z, 1)), "rows", 0, 0, tiled=True, axis_index_groups=Z_GROUPS
    )
    around = shift_y(mine, -1), shift_y(mine, 2), shift_y(mine, 1)
    hi, lo, third_gram, wide = prepare(tensor_slab, third_factor, mine)
    own_gram = call(own_gram_kernel, "own_gram", f32(R, R), (place, mine))
    own_sums = call(own_sums_kernel, "own_sums", f32(R, R), (place, hi, lo, third_factor, mine))

    gram, other = call(
        rest_gram_kernel, "rest_gram", halves, (place, *around, own_gram), SQUARE, (own_sums,)
    )
    gram = gram + swap_core(other)
    sums = call(rest_sums_kernel, "rest_sums", f32(R, R), (place, hi, lo, third_factor, *around, own_sums), (), (gram,))
    gram = gram + swap_x(gram, even)
    sums, other = call(cut_kernel, "cut", halves, (place, sums), (), (gram,))
    gram = gram + swap_x(gram, odd)
    sums = sums + swap_core(other)
    sums = sums + swap_x(sums, even)
    inverse = inverse_start(place, gram, swap_core(gram), third_gram, False, (sums,))
    sums = add(place, sums, swap_x(sums, odd), after=(inverse,))
    inverse = inverse_end(place, inverse, (sums,))
    scaled, chunk, first_own = call(
        first_factor_kernel, "first_factor", [bf16(2 * R, K * R), f32(R // 4, R), f32(32, R)],
        (place, sums, swap_core(sums), inverse, wide), SQUARE * 2,
    )

    sums_of = lambda ahead, *after: call(
        functools.partial(second_sums_kernel, ahead), "second_sums", f32(R, R),
        (place, hi, lo, scaled), (), after,
    )
    far = sums_of(2)
    right = sums_of(1, far)
    chunk = add(place, chunk, shift_y(chunk, 1), shift_y(chunk, -1), shift_y(chunk, 2), after=(right,))
    left = sums_of(3, chunk)
    own = sums_of(0, left)
    below = shift_z(chunk, 1) + chunk
    above = below + shift_z(chunk, -1)
    part_sums = own + shift_y(far, 2) + shift_y(right, 1) + shift_y(left, -1)
    pieces = lax.all_to_all(part_sums, "rows", 0, 0, tiled=True, axis_index_groups=Z_GROUPS)
    chunk = add(place, above, shift_z(above, 3), shift_z(below, -3), after=(part_sums,))
    half = jnp.concatenate([chunk, swap_x(chunk, even)], 0)
    inverse = inverse_start(place, half, swap_core(half), third_gram, True, us=0.7)
    inverse = inverse_end(place, inverse, us=0.7)
    return first_own, call(apply_kernel, "apply", f32(32, R), (place, pieces, inverse))


def solution(mesh):
    return jax.shard_map(
        local,
        mesh=mesh,
        in_specs=(P(None, "rows", "cols"), P(("cols", "rows"), None), P()),
        out_specs=(P(("rows", "cols"), None), P(("cols", "rows"), None)),
        check_vma=False,
    )
```

```python
import functools

import jax
import jax.numpy as jnp
from jax import lax
from jax.experimental import pallas as pl
from jax.experimental.pallas import tpu as pltpu
from jax.sharding import PartitionSpec as P

R = 256
K = 8
B = 64
NB = 16
Y, Z, X = 4, 8, 4
Z_GROUPS = [[y * Z + z for z in range(Z)] for y in range(Y)]


def split3(x):
    a = x.astype(jnp.bfloat16)
    rest = x - a.astype(jnp.float32)
    b = rest.astype(jnp.bfloat16)
    return a, b, (rest - b.astype(jnp.float32)).astype(jnp.bfloat16)


def tdot(x, y):
    x1, x2, x3 = split3(x)
    y1, y2, y3 = split3(y)
    left = jnp.concatenate([x1, x1, x2, x2, x1, x3], 0)
    right = jnp.concatenate([y1, y2, y1, y2, y3, y1], 0)
    return lax.dot_general(
        left, right, (((0,), (0,)), ((), ())), preferred_element_type=jnp.float32
    )


def sweep_columns(columns):
    rows = lax.broadcasted_iota(jnp.int32, (8, 128), 0)
    tiles = range(NB // 8)
    columns = [[c[8 * q : 8 * q + 8] for q in tiles] for c in columns]
    for j in range(NB):
        p, row = divmod(j, 8)
        at = rows == row
        own = columns[j]
        inverse = 1.0 / jnp.broadcast_to(own[p][row : row + 1, :], (8, 128))
        marked = [jnp.where(at, -1.0, own[q]) if q == p else own[q] for q in tiles]
        scaled = [jnp.where(at, -inverse, own[q] * inverse) if q == p else own[q] * inverse for q in tiles]
        after = []
        for k in range(NB):
            if k == j:
                after.append(scaled)
                continue
            entry = jnp.broadcast_to(columns[k][p][row : row + 1, :], (8, 128))
            rest = [jnp.where(at, 0.0, columns[k][q]) if q == p else columns[k][q] for q in tiles]
            if k == j + 1:
                after.append([rest[q] - (marked[q] * entry) * inverse for q in tiles])
            else:
                after.append([rest[q] - scaled[q] * entry for q in tiles])
        columns = after
    return [jnp.concatenate(c, 0) for c in columns]


def tree_sum(terms):
    while len(terms) > 1:
        pairs = [terms[i] + terms[i + 1] for i in range(0, len(terms) - 1, 2)]
        terms = pairs + terms[len(terms) - len(terms) % 2 :]
    return terms[0]


def combine(columns, rows):
    wide = columns[0].shape
    return tree_sum([columns[k] * jnp.broadcast_to(rows[k : k + 1, :], wide) for k in range(NB)])


def invert_block(d):
    lane = lax.broadcasted_iota(jnp.int32, (NB, 128), 1)
    row = lax.broadcasted_iota(jnp.int32, (NB, 128), 0)
    n = B // NB
    d = [d[NB * q : NB * q + NB] for q in range(n)]
    for p in range(n):
        spread = lambda rows: [
            jnp.broadcast_to(rows[:, p * NB + k : p * NB + k + 1], (NB, 128)) for k in range(NB)
        ]
        inside = (lane >= p * NB) & (lane < p * NB + NB)
        panel = jnp.where(inside, jnp.where(lane - p * NB == row, 1.0, 0.0), -d[p])
        y = combine(sweep_columns(spread(d[p])), panel)
        after = {p: y}
        for q in [(p + 1 + i) % n for i in range(n - 1)]:
            after[q] = jnp.where(inside, 0.0, d[q]) - combine(spread(d[q]), y)
        d = [after[q] for q in range(n)]
    return jnp.concatenate(d, 0)


BLOCK, CORE, COL, SIDE = range(4)


def half_rows(place_ref, own):
    core = place_ref[CORE]
    return pl.ds(pl.multiple_of((core if own else 1 - core) * 128, 128), 128)


def eliminate(a_ref, blocks, rows=None):
    lane = lax.broadcasted_iota(jnp.int32, (B, R), 1)
    row = lax.broadcasted_iota(jnp.int32, (B, R), 0)
    lanes = lax.broadcasted_iota(jnp.int32, (R, R), 1)

    def first_lanes(panel, lo):
        block = panel[:, lo // 128 * 128 : lo // 128 * 128 + 128]
        return pltpu.roll(block, 128 - lo % 128, 1) if lo % 128 else block

    panel = a_ref[blocks[0] : blocks[0] + B, :]
    for lo in blocks:
        pivot = invert_block(first_lanes(panel, lo))[:, :B]
        inside = (lane >= lo) & (lane < lo + B)
        y = tdot(pivot, jnp.where(inside, jnp.where(lane - lo == row, 1.0, 0.0), -panel))
        if rows is not None:
            rows = sweep_rows(rows, lo, B, y)
            if lo + B not in blocks:
                return rows
        if lo + B in blocks:
            ahead = first_lanes(panel, lo + B)[:, :B]
            ahead = jnp.where(inside, 0.0, a_ref[lo + B : lo + 2 * B, :]) - tdot(ahead, y)
        a_ref[...] = jnp.where((lanes >= lo) & (lanes < lo + B), 0.0, a_ref[...]) - tdot(panel, y)
        a_ref[lo : lo + B, :] = y
        panel = ahead if lo + B in blocks else None


def sweep_rows(rows, lo, width, y):
    lane = lax.broadcasted_iota(jnp.int32, (32, R), 1)
    half = lo // 128 * 128
    columns = rows[:, half : half + 128].T[lo - half : lo - half + width]
    return jnp.where((lane >= lo) & (lane < lo + width), 0.0, rows) - tdot(columns, y)


def quarter_rows(place_ref, own, first):
    core, side = place_ref[CORE], place_ref[SIDE]
    start = (core if own else 1 - core) * 128 + (side if first else 1 - side) * 64
    return pl.ds(pl.multiple_of(start, 64), 64)


def inverse_start_kernel(quarters, place_ref, own_ref, other_ref, third_ref, out_ref, a_ref):
    for own, ref in ((True, own_ref), (False, other_ref)):
        if quarters:
            for first in (True, False):
                rows = quarter_rows(place_ref, own, first)
                a_ref[rows, :] = ref[0 if first else 64 : 64 if first else 128, :] * third_ref[rows, :]
        else:
            rows = half_rows(place_ref, own)
            a_ref[rows, :] = ref[...] * third_ref[rows, :]
    eliminate(a_ref, range(0, R // 2, B))
    out_ref[...] = a_ref[...]


def inverse_end_kernel(place_ref, half_ref, out_ref, a_ref):
    a_ref[...] = half_ref[...]
    eliminate(a_ref, range(R // 2, R, B))
    out_ref[...] = -a_ref[...]


def f32(*shape):
    return jax.ShapeDtypeStruct(shape, jnp.float32)


def bf16(*shape):
    return jax.ShapeDtypeStruct(shape, jnp.bfloat16)


MICROSECONDS = {
    "own_gram": 1.0, "own_sums": 1.5, "rest_gram": 1.4, "rest_sums": 3.3, "cut": 0.5, "inverse_start": 5.0,
    "inverse_end": 5.0, "first_factor": 1.8, "second_sums": 1.6, "add": 0.5,
    "second_factor": 1.4,
}


def cost(us):
    return pl.CostEstimate(flops=int(us * 1.1e9), bytes_accessed=int(us * 3.6e6), transcendentals=0)


def call(kernel, name, outs, args, scratch=(), after=(), us=None):
    n = len(args)

    def body(*refs):
        kernel(*refs[:n], *refs[n + len(after) :])

    out_specs = jax.tree.map(lambda _: pl.BlockSpec(memory_space=pltpu.VMEM), outs)
    return pl.pallas_call(
        body,
        out_shape=outs,
        in_specs=[pl.BlockSpec(memory_space=pltpu.SMEM)]
        + [pl.BlockSpec(memory_space=pltpu.VMEM)] * (n - 1)
        + [pl.BlockSpec(memory_space=pl.ANY)] * len(after),
        out_specs=out_specs,
        scratch_shapes=list(scratch),
        compiler_params=pltpu.CompilerParams(vmem_limit_bytes=24 * 2**20),
        cost_estimate=cost(us or MICROSECONDS[name]),
        name=name,
    )(*args, *after)


SQUARE = [pltpu.VMEM((R, R), jnp.float32)]


def inverse_start(place, own, other, third_gram, quarters, after=(), us=None):
    return call(functools.partial(inverse_start_kernel, quarters), "inverse_start", f32(R, R), (place, own, other, third_gram), SQUARE, after, us)


def inverse_end(place, half, after=(), us=None):
    return call(inverse_end_kernel, "inverse_end", f32(R, R), (place, half), SQUARE, after, us)


def split2(x):
    a = x.astype(jnp.bfloat16)
    return a, (x - a.astype(jnp.float32)).astype(jnp.bfloat16)


def dot(x, y):
    return jnp.dot(x, y, preferred_element_type=jnp.float32)


def dot6(x, y):
    x1, x2, x3 = split3(x)
    y1, y2, y3 = split3(y)
    return dot(jnp.concatenate([x1, x3, x2, x1, x2, x1], 1), jnp.concatenate([y3, y1, y2, y2, y1, y1], 0))


def prepare_kernel(slab_ref, third_ref, after_ref, hi_ref, lo_ref, gram_ref, wide_ref):
    for block in range(Y):
        hi, lo = split2(slab_ref[0, :, block * R : block * R + R])
        hi_ref[block, 0] = hi
        lo_ref[block, 0] = lo

    @pl.when(pl.program_id(0) == 0)
    def _():
        third = third_ref[...]
        gram_ref[...] = lax.dot_general(
            third, third, (((0,), (0,)), ((), ())), precision=lax.Precision.HIGHEST,
            preferred_element_type=jnp.float32,
        )
        columns = third.T
        for k in range(K):
            wide_ref[k] = jnp.broadcast_to(columns[:, k : k + 1], (R, 128))


def prepare(slab, third, after):
    fixed = lambda *shape: pl.BlockSpec(shape, lambda k: (0,) * len(shape))
    parts = pl.BlockSpec((Y, 1, R, R), lambda k: (0, k, 0, 0))
    return pl.pallas_call(
        prepare_kernel,
        out_shape=[bf16(Y, K, R, R), bf16(Y, K, R, R), f32(R, R), f32(K, R, 128)],
        grid=(K,),
        in_specs=[pl.BlockSpec((1, R, Y * R), lambda k: (k, 0, 0)), fixed(K, R), pl.BlockSpec(memory_space=pl.ANY)],
        out_specs=[parts, parts, fixed(R, R), fixed(K, R, 128)],
        compiler_params=pltpu.CompilerParams(vmem_limit_bytes=24 * 2**20),
        cost_estimate=cost(2.5),
        name="prepare",
    )(slab, third, after)


def first_sums(place_ref, hi_ref, lo_ref, third_ref, blocks, total):
    for ahead, ref in blocks:
        block = lax.rem(place_ref[BLOCK] + ahead, Y)
        hi, lo = split2(ref[...])
        right = jnp.concatenate([hi, hi, lo], 0)
        for k in range(K):
            high, low = hi_ref[block, k], lo_ref[block, k]
            term = dot(jnp.concatenate([high, low, high], 1), right) * third_ref[k : k + 1, :]
            total = term if total is None else total + term
    return total


def own_sums_kernel(place_ref, hi_ref, lo_ref, third_ref, mine_ref, out_ref):
    out_ref[...] = first_sums(place_ref, hi_ref, lo_ref, third_ref, [(0, mine_ref)], None)


def rest_sums_kernel(
    place_ref, hi_ref, lo_ref, third_ref, after_ref, across_ref, before_ref, own_ref, out_ref
):
    blocks = [(1, after_ref), (3, before_ref), (2, across_ref)]
    out_ref[...] = first_sums(place_ref, hi_ref, lo_ref, third_ref, blocks, own_ref[...])


def own_gram_kernel(place_ref, mine_ref, out_ref):
    mine = mine_ref[...]
    out_ref[...] = dot6(mine.T, mine)


def rest_gram_kernel(place_ref, after_ref, across_ref, before_ref, own_ref, out_ref, other_ref, sum_ref):
    total = own_ref[...]
    for ref in (after_ref, before_ref, across_ref):
        block = ref[...]
        total = total + dot6(block.T, block)
    sum_ref[...] = total
    out_ref[...] = sum_ref[half_rows(place_ref, True), :]
    other_ref[...] = sum_ref[half_rows(place_ref, False), :]


def cut_kernel(place_ref, sum_ref, out_ref, other_ref):
    out_ref[...] = sum_ref[half_rows(place_ref, True), :]
    other_ref[...] = sum_ref[half_rows(place_ref, False), :]


def first_factor_kernel(
    place_ref, own_ref, other_ref, inverse_ref, wide_ref, left_ref, chunk_ref, rows_ref, factor_ref, columns_ref
):
    factor_ref[half_rows(place_ref, True), :] = own_ref[...]
    factor_ref[half_rows(place_ref, False), :] = other_ref[...]
    factor = dot6(factor_ref[...], inverse_ref[...])
    factor_ref[...] = factor
    rows_ref[...] = factor_ref[pl.ds(pl.multiple_of(place_ref[COL] * 32, 32), 32), :]
    columns = factor.T
    columns_ref[...] = columns
    chunk_ref[...] = dot6(columns_ref[quarter_rows(place_ref, True, True), :], factor)
    for k in range(K):
        wide = wide_ref[k]
        hi, lo = split2(columns * jnp.concatenate([wide, wide], 1))
        left_ref[:R, k * R : k * R + R] = hi
        left_ref[R:, k * R : k * R + R] = lo


def second_sums_kernel(ahead, place_ref, hi_ref, lo_ref, left_ref, out_ref):
    block = lax.rem(place_ref[BLOCK] + ahead, Y)
    by_hi = dot(left_ref[...], hi_ref[block].reshape(K * R, R))
    by_lo = dot(left_ref[:R, :], lo_ref[block].reshape(K * R, R))
    out_ref[...] = (by_hi[:R] + (by_hi[R:] + by_lo)).T


def add_kernel(place_ref, *refs):
    refs[-1][...] = tree_sum([ref[...] for ref in refs[:-1]])


def add(place, *terms, after=()):
    return call(add_kernel, "add", f32(*terms[0].shape), (place, *terms), (), after)


def second_factor_kernel(place_ref, half_ref, pieces_ref, out_ref, a_ref):
    a_ref[...] = half_ref[...]
    rows = tree_sum([pieces_ref[32 * k : 32 * k + 32, :] for k in range(Z)])
    rows = sweep_rows(rows, 0, R // 2, half_ref[: R // 2, :])
    out_ref[...] = eliminate(a_ref, range(R // 2, R, B), rows)


def shift_y(x, k):
    return lax.ppermute(x, "rows", [(i, (i // Z + k) % Y * Z + i % Z) for i in range(Y * Z)])


def shift_z(x, k):
    return lax.ppermute(x, "rows", [(i, i // Z * Z + (i % Z + k) % Z) for i in range(Y * Z)])


def shift_x(x, k):
    return lax.ppermute(x, "cols", [(i, (i // 2 + k) % X * 2 + i % 2) for i in range(2 * X)])


def swap_x(x, partner):
    return lax.ppermute(x, "cols", [(i, partner[i // 2] * 2 + i % 2) for i in range(2 * X)])


def swap_y(x, partner):
    return lax.ppermute(x, "rows", [(i, partner[i // Z] * Z + i % Z) for i in range(Y * Z)])


def swap_core(x):
    return lax.ppermute(x, "cols", [(i, i ^ 1) for i in range(2 * X)])


def local(tensor_slab, prior_second, third_factor):
    y = lax.axis_index("rows") // Z
    col = lax.axis_index("cols")
    core = col % 2
    place = jnp.stack([y, core, col, col // 2 % 2]).astype(jnp.int32)
    halves = [f32(R // 2, R)] * 2
    even, odd = (1, 0, 3, 2), (3, 2, 1, 0)

    mine = lax.all_to_all(
        jnp.tile(prior_second, (Z, 1)), "rows", 0, 0, tiled=True, axis_index_groups=Z_GROUPS
    )
    around = shift_y(mine, -1), shift_y(mine, 2), shift_y(mine, 1)
    hi, lo, third_gram, wide = prepare(tensor_slab, third_factor, mine)
    own_gram = call(own_gram_kernel, "own_gram", f32(R, R), (place, mine))
    own_sums = call(own_sums_kernel, "own_sums", f32(R, R), (place, hi, lo, third_factor, mine))

    gram, other = call(
        rest_gram_kernel, "rest_gram", halves, (place, *around, own_gram), SQUARE, (own_sums,)
    )
    gram = gram + swap_core(other)
    sums = call(rest_sums_kernel, "rest_sums", f32(R, R), (place, hi, lo, third_factor, *around, own_sums), (), (gram,))
    gram = gram + swap_x(gram, even)
    sums, other = call(cut_kernel, "cut", halves, (place, sums), (), (gram,))
    gram = gram + swap_x(gram, odd)
    sums = sums + swap_core(other)
    sums = sums + swap_x(sums, even)
    inverse = inverse_start(place, gram, swap_core(gram), third_gram, False, (sums,))
    sums = add(place, sums, swap_x(sums, odd), after=(inverse,))
    inverse = inverse_end(place, inverse, (sums,))
    scaled, chunk, first_own = call(
        first_factor_kernel, "first_factor", [bf16(2 * R, K * R), f32(R // 4, R), f32(32, R)],
        (place, sums, swap_core(sums), inverse, wide), SQUARE * 2,
    )

    sums_of = lambda ahead, *after: call(
        functools.partial(second_sums_kernel, ahead), "second_sums", f32(R, R),
        (place, hi, lo, scaled), (), after,
    )
    far = sums_of(2)
    right = sums_of(1, far)
    chunk = add(place, chunk, shift_y(chunk, 1), shift_y(chunk, -1), shift_y(chunk, 2), after=(right,))
    left = sums_of(3, chunk)
    own = sums_of(0, left)
    below = shift_z(chunk, 1) + chunk
    above = below + shift_z(chunk, -1)
    part_sums = own + shift_y(far, 2) + shift_y(right, 1) + shift_y(left, -1)
    pieces = lax.all_to_all(part_sums, "rows", 0, 0, tiled=True, axis_index_groups=Z_GROUPS)
    chunk = add(place, above, shift_z(above, 3), shift_z(below, -3), after=(part_sums,))
    half = jnp.concatenate([chunk, swap_x(chunk, even)], 0)
    inverse = inverse_start(place, half, swap_core(half), third_gram, True, us=1.4)
    return first_own, call(second_factor_kernel, "second_factor", f32(32, R), (place, inverse, pieces), SQUARE)


def solution(mesh):
    return jax.shard_map(
        local,
        mesh=mesh,
        in_specs=(P(None, "rows", "cols"), P(("cols", "rows"), None), P()),
        out_specs=(P(("rows", "cols"), None), P(("cols", "rows"), None)),
        check_vma=False,
    )
```
